256 devices in a mesh: dp: 16 (over x, y_hi, core), tm: 8 (over z), mp: 2 (over y_lo).
Axes of the slice: x: 4, y: 4 (y_hi: 2, y_lo: 2; y = y_hi * 2 + y_lo), z: 8, core: 2. Of those that a mesh axis runs over, the one named last changes fastest.
Arguments:
- query_heads: bfloat16 [16, 16, 256, 2560], P('dp', 'tm', None, 'mp'), may hold values from -4.75 to 4.75
- key_heads: bfloat16 [16, 16, 256, 2560], P('dp', 'tm', None, 'mp'), may hold values from -4.75 to 4.75
- value_heads: bfloat16 [16, 16, 256, 2560], P('dp', 'tm', None, 'mp'), may hold values from -6 to 6
- grad_out: bfloat16 [16, 16, 256, 2560], P('dp', 'tm', None, 'mp'), may hold values from -6 to 6
- out_weight: bfloat16 [2560, 2560], P('dp', 'mp'), may hold values from -0.125 to 0.125
Outputs:
- grad_query: bfloat16 [16, 16, 256, 2560], P('dp', None, 'tm', 'mp')
- grad_key: bfloat16 [16, 16, 256, 2560], P('dp', None, 'tm', 'mp')
- grad_value: bfloat16 [16, 16, 256, 2560], P('dp', None, 'tm', 'mp')
- grad_weight: float32 [2560, 2560], P('dp', 'mp')
The draws below stay inside these ranges and needn't reach their ends.
All inputs are finite; a program needn't handle non-finite values.
Results may differ from the reference program's by a relative error of at most 0.0058.
Values may be sent and summed in bfloat16 or wider, within the bound.
A program may use at most 128 MiB of HBM per device.

```python
import jax
import jax.numpy as jnp
from jax import lax

OUT = 2560
HEADS = 20
HS = 128
FRAMES = 16
PATCHES = 256
TRAJ = 16
HH = 2560


def draw_query_heads(key, part):
    key = jax.random.fold_in(key, 11)
    full_shape = (TRAJ, FRAMES, PATCHES, HEADS * HS)
    entries = jnp.clip(jax.random.normal(key, full_shape), -4.5, 4.5)
    return entries.astype(jnp.bfloat16)


def draw_key_heads(key, part):
    key = jax.random.fold_in(key, 23)
    full_shape = (TRAJ, FRAMES, PATCHES, HEADS * HS)
    entries = jnp.clip(jax.random.normal(key, full_shape), -4.5, 4.5)
    return entries.astype(jnp.bfloat16)


def strengthened(values, key, source, target, blocks, factor):
    def block_of(axis_at):
        return (jnp.arange(values.shape[axis_at]) // (values.shape[axis_at] // blocks)).reshape((-1,) + (1,) * (values.ndim - 1 - axis_at))

    first = jax.random.permutation(key, blocks)[block_of(target)]
    other_side = (block_of(target) + blocks // 2) % blocks
    return jnp.where((block_of(source) == first) | (block_of(source) == other_side), factor * values, values)


def shard_levels(rng, dims, pieces, low, high):
    factor_of, own = 1.0, jax.random.fold_in(rng, 6)
    for axis_at, parts in pieces:
        draws = jnp.exp(jax.random.uniform(jax.random.fold_in(own, axis_at), (parts,), jnp.float32, low / len(pieces), high / len(pieces)))
        factor_of = factor_of * jnp.repeat(draws, dims[axis_at] // parts).reshape([-1 if axis == axis_at else 1 for axis in range(len(dims))])
    return factor_of


def bell_draw(rng, shape, width, limit, cuts=(), held_as=jnp.bfloat16):
    drawn = width * jax.random.normal(rng, shape, jnp.float32)
    if cuts:
        drawn = drawn * shard_levels(rng, shape, cuts, -0.22, 0.18)
    return jnp.clip(drawn, -limit, limit).astype(held_as)


def bell_draw_with(rng, shape, scale, reach, cuts, heavy, dtype=jnp.bfloat16):
    drawn = scale * jax.random.normal(rng, shape, jnp.float32)
    if cuts:
        drawn = drawn * shard_levels(rng, shape, cuts, -0.22, 0.18)
    return jnp.clip(strengthened(drawn, jax.random.fold_in(rng, 3), *heavy), -reach, reach).astype(dtype)


def setup_inputs(seed: int = 0) -> dict:
    key_of = jax.random.split(jax.random.key(seed), 6)
    query_heads = draw_query_heads(jax.random.fold_in(key_of[5], 71), 0)
    key_heads = draw_key_heads(jax.random.fold_in(key_of[5], 71), 0)
    value_heads = bell_draw(key_of[2], (TRAJ, FRAMES, PATCHES, HH), 1.0, 6.0, ((0, 16), (1, 8), (3, 2)))
    grad_out = bell_draw_with(key_of[3], (TRAJ, FRAMES, PATCHES, OUT), 1.0, 6.0, ((0, 16), (1, 8), (3, 2)), (0, 3, 16, 2.0))
    out_weight = bell_draw(key_of[4], (OUT, HH), OUT ** -0.5, 0.125, ((0, 16), (1, 2)))
    return dict(query_heads=query_heads, key_heads=key_heads, value_heads=value_heads, grad_out=grad_out, out_weight=out_weight)


def attend_back(query_part, key_part, value_part, grad_part):
    frame_count = query_part.shape[0]
    score_scale = HS ** -0.5
    query_wide = query_part.astype(jnp.float32)
    key_wide = key_part.astype(jnp.float32)
    value_wide = value_part.astype(jnp.float32)
    grad_wide = grad_part.astype(jnp.float32)
    scores = jnp.einsum("iphs,jphs->phij", query_wide, key_wide) * score_scale
    causal = jnp.arange(frame_count)[:, None] >= jnp.arange(frame_count)[None, :]
    scores = jnp.where(causal, scores, jnp.float32(-1e30))
    highest = jnp.max(scores, axis=-1, keepdims=True)
    weights = jnp.exp(scores - highest)
    probs = weights / jnp.sum(weights, axis=-1, keepdims=True)
    probs_low = lax.optimization_barrier(probs.astype(jnp.bfloat16)).astype(jnp.float32)
    attended = jnp.einsum("phij,jphs->iphs", probs_low, value_wide).astype(jnp.bfloat16)
    d_probs = jnp.einsum("iphs,jphs->phij", grad_wide, value_wide)
    row_inner = jnp.sum(probs * d_probs, axis=-1, keepdims=True)
    d_scores = lax.optimization_barrier((probs * (d_probs - row_inner)).astype(jnp.bfloat16)).astype(jnp.float32)
    grad_query = (jnp.einsum("phij,jphs->iphs", d_scores, key_wide) * score_scale).astype(jnp.bfloat16)
    grad_key = (jnp.einsum("phij,iphs->jphs", d_scores, query_wide) * score_scale).astype(jnp.bfloat16)
    grad_value = jnp.einsum("phij,iphs->jphs", probs_low, grad_wide).astype(jnp.bfloat16)
    return grad_query, grad_key, grad_value, attended


def reference(query_heads, key_heads, value_heads, grad_out, out_weight):
    token_rows = grad_out.reshape(-1, OUT)
    d_attended = jnp.dot(token_rows, out_weight, preferred_element_type=jnp.float32).astype(jnp.bfloat16)
    split_shape = (TRAJ, FRAMES, PATCHES, HEADS, HS)

    def one_window(operands):
        return attend_back(*operands)

    grad_query, grad_key, grad_value, attended = lax.map(one_window, (query_heads.reshape(split_shape), key_heads.reshape(split_shape), value_heads.reshape(split_shape), d_attended.reshape(split_shape)))
    grad_weight = jnp.dot(token_rows.T, attended.reshape(-1, HEADS * HS), preferred_element_type=jnp.float32)
    grad_weight = grad_weight * ((TRAJ * FRAMES * PATCHES) ** -0.5)
    whole_shape = (TRAJ, FRAMES, PATCHES, HEADS * HS)
    return grad_query.reshape(whole_shape), grad_key.reshape(whole_shape), grad_value.reshape(whole_shape), grad_weight
```

```python
import functools

import jax
import jax.numpy as jnp
from jax import lax
from jax.experimental import pallas as pl
from jax.experimental.pallas import tpu as pltpu
from jax.sharding import PartitionSpec as P

HS = 128
MESH = pl.DeviceIdType.MESH
GROUP = 2
WIDE = GROUP * HS


def kernel(
    dims, query, key, value, grad, weight,
    dq_out, dk_out, dv_out, gw_out,
    G, GT, W, QKV, OUT, DA, ATT, PR, BIAS, CSEND, CRECV, OWN, XSEND, XRECV, ZSEND, ZRECV, ZALL, GW,
    g_send, g_recv, gy_send, gy_recv, w_send, w_recv, wf_send, wf_recv, q_send, q_recv,
    own_g, own_w, own_q, c_send, c_recv, x_send, x_recv, zr_send, zr_recv, za_send, za_recv, out_sem, gw_sem,
):
    groups, grad_scale = dims
    dp, z, m = lax.axis_index("dp"), lax.axis_index("tm"), lax.axis_index("mp")
    c, xh = lax.rem(dp, 2), dp // 2
    sibling = (dp + 1 - 2 * c, z, m)
    partner = (dp, z, 1 - m)

    def z_peer(d):
        return lax.rem(z + d, 8)

    def x_peer(d):
        return lax.rem(xh + d, 8)

    def drain(ref, sem):
        pltpu.make_async_copy(ref, ref, sem).wait()

    def remote(src, dst, ss, rs, to):
        pltpu.make_async_remote_copy(
            src_ref=src, dst_ref=dst, send_sem=ss, recv_sem=rs, device_id=to, device_id_type=MESH
        ).start()

    barrier = pltpu.get_barrier_semaphore()
    for to in [sibling, partner]:
        pl.semaphore_signal(barrier, inc=1, device_id=to, device_id_type=MESH)

    def greet(d, _):
        pl.semaphore_signal(barrier, inc=1, device_id=(dp, z_peer(d), m), device_id_type=MESH)
        pl.semaphore_signal(barrier, inc=1, device_id=(x_peer(d) * 2 + c, z, m), device_id_type=MESH)
        return 0

    lax.fori_loop(1, 8, greet, 0)
    mine = pl.ds(pl.multiple_of(z * 32, 32), 32)
    frames = pl.ds(2 * z, 2)
    pltpu.make_async_copy(grad.at[0, :, mine], G.at[m, frames], own_g).start()
    pltpu.make_async_copy(weight, W.at[xh, c], own_w).start()
    for a, src in enumerate((query, key, value)):
        pltpu.make_async_copy(src.at[0, :, mine], QKV.at[a, frames], own_q).start()
    pl.semaphore_wait(barrier, 16)

    order = (1, 7, 2, 6, 3, 5, 4)

    for i, d in enumerate(order):
        zz = z_peer(d)
        remote(
            grad.at[0, :, pl.ds(pl.multiple_of(zz * 32, 32), 32)], G.at[m, frames], g_send, g_recv.at[i], (dp, zz, m)
        )
    remote(grad.at[0, :, mine], G.at[m, frames], gy_send, gy_recv, partner)

    def send_w(d, _):
        remote(weight, W.at[xh, c], w_send, w_recv, (x_peer(d) * 2 + c, z, m))
        return 0

    lax.fori_loop(1, 8, send_w, 0)

    def send_group(k):
        cols = pl.ds(pl.multiple_of(k * WIDE, WIDE), WIDE)
        for d in order:
            zz = z_peer(d)
            rows = pl.ds(pl.multiple_of(zz * 32, 32), 32)
            for a, src in enumerate((query, key, value)):
                remote(
                    src.at[0, :, rows, cols], QKV.at[a, frames, :, cols], q_send.at[k], q_recv.at[k], (dp, zz, m)
                )

    send_group(0)
    row = lax.broadcasted_iota(jnp.int32, (256, 256), 0)
    col = lax.broadcasted_iota(jnp.int32, (256, 256), 1)
    BIAS[...] = jnp.where((lax.rem(row, 16) == lax.rem(col, 16)) & (col <= row), 0.0, -1e30).astype(jnp.float32)
    ZSEND[:, pl.ds(10 * GROUP, 24 - 10 * GROUP)] = jnp.zeros((groups, 24 - 10 * GROUP, 16, 128), jnp.bfloat16)

    for i, d in enumerate(order):
        zz = lax.rem(z + 8 - d, 8)
        there = G.at[m, pl.ds(2 * zz, 2)]
        drain(there, g_recv.at[i])
        remote(there, there, gy_send, gy_recv, partner)
    send_group(1)
    drain(grad.at[0, :, mine], own_g)

    def turn(half):
        def body(j, _):
            lanes = pl.ds(pl.multiple_of(j * 128, 128), 128)
            block = G[half, :, :, lanes].reshape(512, 128)
            GT[pl.ds(pl.multiple_of(half * 1280 + j * 128, 128), 128), :] = block.T
            return 0

        lax.fori_loop(0, 10, body, 0)

    turn(m)
    drain(W.at[pl.ds(0, 7), c], w_recv)
    drain(weight, own_w)
    remote(W.at[:, c], W.at[:, c], wf_send, wf_recv, sibling)
    drain(G.at[1 - m], gy_recv)
    turn(1 - m)
    drain(W.at[:, 1 - c], wf_recv)
    for a in range(1):
        drain(QKV.at[:, frames], own_q)

    def block_of(ref, b, lanes):
        return ref[:, pl.ds(16 * b, 16), lanes].reshape(256, HS)

    def rows_for(core):
        return jnp.concatenate(
            [GT[pl.ds(pl.multiple_of((2 * s + core) * 160, 32), 160), :] for s in range(8)], axis=0
        )

    def finish_xy(k):
        drain(XRECV.at[k, pl.ds(0, 7)], x_recv.at[k])
        total = XSEND[k, xh].astype(jnp.float32)
        for d in range(1, 8):
            total = total + XRECV[k, x_peer(d)].astype(jnp.float32)
        for h in range(GROUP):
            ZSEND[k, pl.ds(10 * h, 10)] = total[:, h * HS:(h + 1) * HS].astype(jnp.bfloat16).reshape(10, 16, 128)

        def send(d, _):
            zz = z_peer(d)
            remote(ZSEND.at[k, pl.ds(3 * zz, 3)], ZRECV.at[k, z], zr_send.at[k], zr_recv.at[k], (dp, zz, m))
            return 0

        lax.fori_loop(1, 8, send, 0)

    def finish_z(k):
        drain(ZRECV.at[k, pl.ds(0, 7)], zr_recv.at[k])
        total = ZSEND[k, pl.ds(3 * z, 3)].astype(jnp.float32)
        for d in range(1, 8):
            total = total + ZRECV[k, z_peer(d)].astype(jnp.float32)
        ZALL[k, pl.ds(3 * z, 3)] = total.astype(jnp.bfloat16)

        def send(d, _):
            here = ZALL.at[k, pl.ds(3 * z, 3)]
            remote(here, here, za_send.at[k], za_recv.at[k], (dp, z_peer(d), m))
            return 0

        lax.fori_loop(1, 8, send, 0)

    def step(k, _):
        cols = pl.ds(pl.multiple_of(k * WIDE, WIDE), WIDE)
        drain(QKV.at[:, pl.ds(0, 14), :, cols], q_recv.at[k])

        @pl.when(k + 2 < groups)
        def _():
            send_group(k + 2)

        for h in range(GROUP):
            lanes = pl.ds(pl.multiple_of(k * WIDE + h * HS, HS), HS)
            for b in range(2):
                q = block_of(QKV.at[0], b, lanes)
                kk = block_of(QKV.at[1], b, lanes)
                v = block_of(QKV.at[2], b, lanes)
                s = lax.dot_general(q, kk, (((1,), (1,)), ((), ())), preferred_element_type=jnp.float32)
                s = s * (HS ** -0.5) + BIAS[...]
                e = jnp.exp(s - jnp.max(s, axis=-1, keepdims=True))
                p = e / jnp.sum(e, axis=-1, keepdims=True)
                PR[2 * h + b] = p
                att = jnp.dot(p.astype(jnp.bfloat16), v, preferred_element_type=jnp.float32).astype(jnp.bfloat16)
                ATT[:, pl.ds(16 * b, 16), pl.ds(h * HS, HS)] = att.reshape(16, 16, HS)

        att = ATT[...].reshape(512, WIDE)
        theirs = jnp.dot(rows_for(1 - c), att, preferred_element_type=jnp.float32)
        CSEND[k] = theirs.astype(jnp.bfloat16).reshape(8, 160, WIDE)
        remote(CSEND.at[k], CRECV.at[k], c_send.at[k], c_recv.at[k], sibling)
        OWN[...] = jnp.dot(rows_for(c), att, preferred_element_type=jnp.float32).reshape(8, 160, WIDE)

        da = jnp.dot(
            G[0].reshape(512, 1280), W[pl.ds(0, 4), :, :, cols].reshape(1280, WIDE), preferred_element_type=jnp.float32
        )
        da = da + jnp.dot(
            G[1].reshape(512, 1280), W[pl.ds(4, 4), :, :, cols].reshape(1280, WIDE), preferred_element_type=jnp.float32
        )
        DA[...] = da.astype(jnp.bfloat16).reshape(16, 32, WIDE)

        for h in range(GROUP):
            lanes = pl.ds(pl.multiple_of(k * WIDE + h * HS, HS), HS)
            for b in range(2):
                q = block_of(QKV.at[0], b, lanes)
                kk = block_of(QKV.at[1], b, lanes)
                v = block_of(QKV.at[2], b, lanes)
                d_att = block_of(DA, b, pl.ds(h * HS, HS))
                p = PR[2 * h + b]
                dp_ = lax.dot_general(d_att, v, (((1,), (1,)), ((), ())), preferred_element_type=jnp.float32)
                inner = jnp.sum(p * dp_, axis=-1, keepdims=True)
                ds = (p * (dp_ - inner)).astype(jnp.bfloat16)
                over_rows = (((0,), (0,)), ((), ()))
                dq = jnp.dot(ds, kk, preferred_element_type=jnp.float32) * (HS ** -0.5)
                dk = lax.dot_general(ds, q, over_rows, preferred_element_type=jnp.float32) * (HS ** -0.5)
                dv = lax.dot_general(p.astype(jnp.bfloat16), d_att, over_rows, preferred_element_type=jnp.float32)
                for a, r in enumerate((dq, dk, dv)):
                    OUT[a, :, pl.ds(16 * b, 16), lanes] = r.astype(jnp.bfloat16).reshape(16, 16, HS)
        for a, dst in enumerate((dq_out, dk_out, dv_out)):
            pltpu.make_async_copy(OUT.at[a, :, :, cols], dst.at[0, :, :, cols], out_sem).start()

        drain(CRECV.at[k], c_recv.at[k])
        for s in range(8):
            XSEND[k, s] = (OWN[s] + CRECV[k, s].astype(jnp.float32)).astype(jnp.bfloat16)

        def send(d, _):
            to = x_peer(d)
            remote(XSEND.at[k, to], XRECV.at[k, xh], x_send.at[k], x_recv.at[k], (to * 2 + c, z, m))
            return 0

        lax.fori_loop(1, 8, send, 0)

        @pl.when(k >= 1)
        def _():
            finish_xy(k - 1)

        @pl.when(k >= 2)
        def _():
            finish_z(k - 2)

        return 0

    lax.fori_loop(0, groups, step, 0)
    finish_z(groups - 2)
    finish_xy(groups - 1)
    finish_z(groups - 1)

    def place(k, _):
        drain(ZALL.at[k, pl.ds(0, 21)], za_recv.at[k])
        for h in range(GROUP):
            lanes = pl.ds(pl.multiple_of(k * WIDE + h * HS, HS), HS)
            GW[:, lanes] = ZALL[k, pl.ds(10 * h, 10)].astype(jnp.float32).reshape(160, 128) * grad_scale
        return 0

    lax.fori_loop(0, groups, place, 0)
    last = pltpu.make_async_copy(GW, gw_out, gw_sem)
    last.start()

    drain(G.at[m, pl.ds(0, 14)], g_send)
    drain(G.at[m], gy_send)
    drain(W.at[pl.ds(0, 7), c], w_send)
    drain(W.at[:, c], wf_send)

    def settle(k, _):
        cols = pl.ds(pl.multiple_of(k * WIDE, WIDE), WIDE)
        drain(QKV.at[:, pl.ds(0, 14), :, cols], q_send.at[k])
        drain(CSEND.at[k], c_send.at[k])
        drain(XSEND.at[k, pl.ds(0, 7)], x_send.at[k])
        drain(ZRECV.at[k, pl.ds(0, 7)], zr_send.at[k])
        drain(ZALL.at[k, pl.ds(0, 21)], za_send.at[k])
        return 0

    lax.fori_loop(0, groups, settle, 0)
    drain(OUT, out_sem)
    last.wait()


def on_device(query_heads, key_heads, value_heads, grad_out, out_weight):
    groups = query_heads.shape[3] // WIDE
    bf, f32 = jnp.bfloat16, jnp.float32
    dma, vmem = pltpu.SemaphoreType.DMA, pltpu.VMEM
    anywhere = pl.BlockSpec(memory_space=pl.ANY)
    part = jax.ShapeDtypeStruct((1, 16, 32, 1280), bf)
    return pl.pallas_call(
        functools.partial(kernel, (groups, float(16 * 16 * 256) ** -0.5)),
        out_shape=(part, part, part, jax.ShapeDtypeStruct((160, 1280), f32)),
        in_specs=[anywhere] * 5,
        out_specs=(anywhere,) * 4,
        scratch_shapes=[
            vmem((2, 16, 32, 1280), bf),
            vmem((2560, 512), bf),
            vmem((8, 2, 160, 1280), bf),
            vmem((3, 16, 32, 1280), bf),
            vmem((3, 16, 32, 1280), bf),
            vmem((16, 32, WIDE), bf),
            vmem((16, 32, WIDE), bf),
            vmem((2 * GROUP, 256, 256), f32),
            vmem((256, 256), f32),
            vmem((groups, 8, 160, WIDE), bf),
            vmem((groups, 8, 160, WIDE), bf),
            vmem((8, 160, WIDE), f32),
            vmem((groups, 8, 160, WIDE), bf),
            vmem((groups, 8, 160, WIDE), bf),
            vmem((groups, 24, 16, 128), bf),
            vmem((groups, 8, 3, 16, 128), bf),
            vmem((groups, 24, 16, 128), bf),
            vmem((160, 1280), f32),
            dma, dma((7,)), dma, dma, dma, dma, dma, dma, dma((groups,)), dma((groups,)),
            dma, dma, dma, dma((groups,)), dma((groups,)), dma((groups,)), dma((groups,)),
            dma((groups,)), dma((groups,)), dma((groups,)), dma((groups,)), dma, dma,
        ],
        compiler_params=pltpu.CompilerParams(
            collective_id=0, has_side_effects=True, vmem_limit_bytes=58 * 2**20
        ),
    )(query_heads, key_heads, value_heads, grad_out, out_weight)


def solution(mesh):
    placed = (
        P("dp", "tm", None, "mp"),
        P("dp", "tm", None, "mp"),
        P("dp", "tm", None, "mp"),
        P("dp", "tm", None, "mp"),
        P("dp", "mp"),
    )
    return jax.shard_map(
        on_device,
        mesh=mesh,
        in_specs=placed,
        out_specs=(
            P("dp", None, "tm", "mp"),
            P("dp", None, "tm", "mp"),
            P("dp", None, "tm", "mp"),
            P("dp", "mp"),
        ),
        check_vma=False,
    )
```

```python
import functools

import jax
import jax.numpy as jnp
from jax import lax
from jax.experimental import pallas as pl
from jax.experimental.pallas import tpu as pltpu
from jax.sharding import PartitionSpec as P

HS = 128
MESH = pl.DeviceIdType.MESH
GROUP = 2
WIDE = GROUP * HS
OWNED = -(-10 * GROUP // 8)


def kernel(
    dims, query, key, value, grad, weight,
    dq_out, dk_out, dv_out, GW,
    G, GT, W, QKV, DA, ATT, PR, BIAS, CSEND, CRECV, OWN, XSEND, XRECV, ASEND, ARECV, AALL, BSEND, BRECV, BALL,
    g_send, g_recv, gy_send, gy_recv, wh_send, wh_recv, w_send, w_recv, wf_send, wf_recv, q_send, q_recv,
    own_g, own_w, own_q, c_send, c_recv, x_send, x_recv, ar_send, ar_recv, ag_send, ag_recv, br_send, br_recv, bg_send, bg_recv,
):
    groups, grad_scale = dims
    dp, z, m = lax.axis_index("dp"), lax.axis_index("tm"), lax.axis_index("mp")
    c, xh = lax.rem(dp, 2), dp // 2
    sibling = (dp + 1 - 2 * c, z, m)
    partner = (dp, z, 1 - m)

    def z_peer(d):
        return lax.rem(z + d, 8)

    def x_peer(d):
        return lax.rem(xh + d, 8)

    def drain(ref, sem):
        pltpu.make_async_copy(ref, ref, sem).wait()

    def remote(src, dst, ss, rs, to):
        pltpu.make_async_remote_copy(
            src_ref=src, dst_ref=dst, send_sem=ss, recv_sem=rs, device_id=to, device_id_type=MESH
        ).start()

    barrier = pltpu.get_barrier_semaphore()
    for to in [sibling, partner]:
        pl.semaphore_signal(barrier, inc=1, device_id=to, device_id_type=MESH)

    def greet(d, _):
        pl.semaphore_signal(barrier, inc=1, device_id=(dp, z_peer(d), m), device_id_type=MESH)
        pl.semaphore_signal(barrier, inc=1, device_id=(x_peer(d) * 2 + c, z, m), device_id_type=MESH)
        return 0

    lax.fori_loop(1, 8, greet, 0)
    mine = pl.ds(pl.multiple_of(z * 32, 32), 32)
    frames = pl.ds(2 * z, 2)
    pltpu.make_async_copy(grad.at[0, :, mine], G.at[m, frames], own_g).start()
    pltpu.make_async_copy(weight, W.at[xh, c], own_w).start()
    for a, src in enumerate((query, key, value)):
        pltpu.make_async_copy(src.at[0, :, mine], QKV.at[a, frames], own_q).start()
    pl.semaphore_wait(barrier, 16)

    order = (1, 7, 2, 6, 3, 5, 4)

    for i, d in enumerate(order):
        zz = z_peer(d)
        remote(
            grad.at[0, :, pl.ds(pl.multiple_of(zz * 32, 32), 32)], G.at[m, frames], g_send, g_recv.at[i], (dp, zz, m)
        )
    remote(grad.at[0, :, mine], G.at[m, frames], gy_send, gy_recv, partner)

    other = xh + 1 - 2 * lax.rem(xh, 2)
    remote(weight, W.at[xh, c], wh_send, wh_recv, (other * 2 + c, z, m))

    def send_w(src, slot):
        for d in (2, 6, 4):
            remote(src, W.at[slot, c], w_send, w_recv, (x_peer(d) * 2 + c, z, m))

    send_w(weight, xh)

    def send_group(k):
        cols = pl.ds(pl.multiple_of(k * WIDE, WIDE), WIDE)
        for d in order:
            zz = z_peer(d)
            rows = pl.ds(pl.multiple_of(zz * 32, 32), 32)
            for a, src in enumerate((query, key, value)):
                remote(
                    src.at[0, :, rows, cols], QKV.at[a, frames, :, cols], q_send.at[k], q_recv.at[k], (dp, zz, m)
                )

    send_group(0)
    row = lax.broadcasted_iota(jnp.int32, (256, 256), 0)
    col = lax.broadcasted_iota(jnp.int32, (256, 256), 1)
    BIAS[...] = jnp.where((lax.rem(row, 16) == lax.rem(col, 16)) & (col <= row), 0.0, -1e30).astype(jnp.float32)
    BSEND[...] = jnp.zeros(BSEND.shape, jnp.bfloat16)

    for i, d in enumerate(order):
        zz = lax.rem(z + 8 - d, 8)
        there = G.at[m, pl.ds(2 * zz, 2)]
        drain(there, g_recv.at[i])
        remote(there, there, gy_send, gy_recv, partner)
        if i == 1:
            drain(weight, wh_recv)
            send_w(W.at[other, c], other)
    send_group(1)
    drain(grad.at[0, :, mine], own_g)

    def turn(half):
        def body(j, _):
            lanes = pl.ds(pl.multiple_of(j * 128, 128), 128)
            block = G[half, :, :, lanes].reshape(512, 128)
            GT[pl.ds(pl.multiple_of(half * 1280 + j * 128, 128), 128), :] = block.T
            return 0

        lax.fori_loop(0, 10, body, 0)

    turn(m)
    drain(W.at[pl.ds(0, 6), c], w_recv)
    drain(weight, own_w)
    remote(W.at[:, c], W.at[:, c], wf_send, wf_recv, sibling)
    drain(G.at[1 - m], gy_recv)
    turn(1 - m)
    drain(QKV.at[:, frames], own_q)

    def block_of(ref, b, lanes):
        return ref[:, pl.ds(16 * b, 16), lanes].reshape(256, HS)

    def rows_for(core):
        return jnp.concatenate(
            [GT[pl.ds(pl.multiple_of((2 * s + core) * 160, 32), 160), :] for s in range(8)], axis=0
        )

    def sum_xy(k):
        drain(XRECV.at[k, pl.ds(0, 7)], x_recv.at[k])
        total = XSEND[k, xh].astype(jnp.float32)
        for d in range(1, 8):
            total = total + XRECV[k, x_peer(d)].astype(jnp.float32)
        return [total[:, h * HS:(h + 1) * HS].astype(jnp.bfloat16) for h in range(GROUP)]

    def scatter_z(src, dst, ss, rs):
        def send(d, _):
            zz = z_peer(d)
            remote(src.at[zz], dst.at[z], ss, rs, (dp, zz, m))
            return 0

        lax.fori_loop(1, 8, send, 0)

    def gather_z(src, dst, all_, rs, ss, gs):
        drain(dst.at[pl.ds(0, 7)], rs)
        total = src[z].astype(jnp.float32)
        for d in range(1, 8):
            total = total + dst[z_peer(d)].astype(jnp.float32)
        all_[z] = total.astype(jnp.bfloat16)

        def send(d, _):
            remote(all_.at[z], all_.at[z], ss, gs, (dp, z_peer(d), m))
            return 0

        lax.fori_loop(1, 8, send, 0)

    def step(k, _):
        cols = pl.ds(pl.multiple_of(k * WIDE, WIDE), WIDE)
        drain(QKV.at[:, pl.ds(0, 14), :, cols], q_recv.at[k])

        @pl.when(k + 2 < groups)
        def _():
            send_group(k + 2)

        for h in range(GROUP):
            lanes = pl.ds(pl.multiple_of(k * WIDE + h * HS, HS), HS)
            for b in range(2):
                q = block_of(QKV.at[0], b, lanes)
                kk = block_of(QKV.at[1], b, lanes)
                v = block_of(QKV.at[2], b, lanes)
                s = lax.dot_general(q, kk, (((1,), (1,)), ((), ())), preferred_element_type=jnp.float32)
                s = s * (HS ** -0.5) + BIAS[...]
                e = jnp.exp(s - jnp.max(s, axis=-1, keepdims=True))
                p = e / jnp.sum(e, axis=-1, keepdims=True)
                PR[2 * h + b] = p
                att = jnp.dot(p.astype(jnp.bfloat16), v, preferred_element_type=jnp.float32).astype(jnp.bfloat16)
                ATT[:, pl.ds(16 * b, 16), pl.ds(h * HS, HS)] = att.reshape(16, 16, HS)

        att = ATT[...].reshape(512, WIDE)
        theirs = jnp.dot(rows_for(1 - c), att, preferred_element_type=jnp.float32)
        CSEND[k] = theirs.astype(jnp.bfloat16).reshape(8, 160, WIDE)
        remote(CSEND.at[k], CRECV.at[k], c_send.at[k], c_recv.at[k], sibling)
        OWN[...] = jnp.dot(rows_for(c), att, preferred_element_type=jnp.float32).reshape(8, 160, WIDE)

        @pl.when(k >= 1)
        def _():
            for h, part in enumerate(sum_xy(k - 1)):
                ASEND[GROUP * (k - 1) + h] = part

        @pl.when(k == groups - 1)
        def _():
            scatter_z(ASEND, ARECV, ar_send, ar_recv)

        @pl.when(k == 0)
        def _():
            drain(W.at[:, 1 - c], wf_recv)

        da = jnp.dot(
            G[0].reshape(512, 1280), W[pl.ds(0, 4), :, :, cols].reshape(1280, WIDE), preferred_element_type=jnp.float32
        )
        da = da + jnp.dot(
            G[1].reshape(512, 1280), W[pl.ds(4, 4), :, :, cols].reshape(1280, WIDE), preferred_element_type=jnp.float32
        )
        DA[...] = da.astype(jnp.bfloat16).reshape(16, 32, WIDE)

        drain(CRECV.at[k], c_recv.at[k])
        for s in range(8):
            XSEND[k, s] = (OWN[s] + CRECV[k, s].astype(jnp.float32)).astype(jnp.bfloat16)

        def send(d, _):
            to = x_peer(d)
            remote(XSEND.at[k, to], XRECV.at[k, xh], x_send.at[k], x_recv.at[k], (to * 2 + c, z, m))
            return 0

        lax.fori_loop(1, 8, send, 0)

        for h in range(GROUP):
            lanes = pl.ds(pl.multiple_of(k * WIDE + h * HS, HS), HS)
            for b in range(2):
                q = block_of(QKV.at[0], b, lanes)
                kk = block_of(QKV.at[1], b, lanes)
                v = block_of(QKV.at[2], b, lanes)
                d_att = block_of(DA, b, pl.ds(h * HS, HS))
                p = PR[2 * h + b]
                dp_ = lax.dot_general(d_att, v, (((1,), (1,)), ((), ())), preferred_element_type=jnp.float32)
                inner = jnp.sum(p * dp_, axis=-1, keepdims=True)
                ds = (p * (dp_ - inner)).astype(jnp.bfloat16)
                over_rows = (((0,), (0,)), ((), ()))
                dq = jnp.dot(ds, kk, preferred_element_type=jnp.float32) * (HS ** -0.5)
                dk = lax.dot_general(ds, q, over_rows, preferred_element_type=jnp.float32) * (HS ** -0.5)
                dv = lax.dot_general(p.astype(jnp.bfloat16), d_att, over_rows, preferred_element_type=jnp.float32)
                for dst, r in ((dq_out, dq), (dk_out, dk), (dv_out, dv)):
                    dst[0, :, pl.ds(16 * b, 16), lanes] = r.astype(jnp.bfloat16).reshape(16, 16, HS)

        return 0

    lax.fori_loop(0, groups, step, 0)
    gather_z(ASEND, ARECV, AALL, ar_recv, ag_send, ag_recv)
    for h, part in enumerate(sum_xy(groups - 1)):
        for t in range(10):
            at = 10 * h + t
            BSEND[at // OWNED, at % OWNED] = part[16 * t:16 * t + 16]
    scatter_z(BSEND, BRECV, br_send, br_recv)
    drain(AALL.at[pl.ds(0, 7)], ag_recv)
    for u in range(8):
        GW[:, u * HS:(u + 1) * HS] = AALL[u].astype(jnp.float32) * grad_scale
    gather_z(BSEND, BRECV, BALL, br_recv, bg_send, bg_recv)
    drain(BALL.at[pl.ds(0, 7)], bg_recv)
    for h in range(GROUP):
        for t in range(10):
            at = 10 * h + t
            lanes = pl.ds((8 + h) * HS, HS)
            GW[16 * t:16 * t + 16, lanes] = BALL[at // OWNED, at % OWNED].astype(jnp.float32) * grad_scale

    drain(G.at[m, pl.ds(0, 14)], g_send)
    drain(G.at[m], gy_send)
    drain(weight, wh_send)
    drain(W.at[pl.ds(0, 6), c], w_send)
    drain(W.at[:, c], wf_send)

    def settle(k, _):
        cols = pl.ds(pl.multiple_of(k * WIDE, WIDE), WIDE)
        drain(QKV.at[:, pl.ds(0, 14), :, cols], q_send.at[k])
        drain(CSEND.at[k], c_send.at[k])
        drain(XSEND.at[k, pl.ds(0, 7)], x_send.at[k])
        return 0

    lax.fori_loop(0, groups, settle, 0)
    drain(ARECV.at[pl.ds(0, 7)], ar_send)
    drain(ARECV.at[pl.ds(0, 7)], ag_send)
    drain(BRECV.at[pl.ds(0, 7)], br_send)
    drain(BRECV.at[pl.ds(0, 7)], bg_send)


def on_device(query_heads, key_heads, value_heads, grad_out, out_weight):
    groups = query_heads.shape[3] // WIDE
    bf, f32 = jnp.bfloat16, jnp.float32
    dma, vmem = pltpu.SemaphoreType.DMA, pltpu.VMEM
    anywhere = pl.BlockSpec(memory_space=pltpu.HBM)
    part = jax.ShapeDtypeStruct((1, 16, 32, 1280), bf)
    return pl.pallas_call(
        functools.partial(kernel, (groups, float(16 * 16 * 256) ** -0.5)),
        out_shape=(part, part, part, jax.ShapeDtypeStruct((160, 1280), f32)),
        in_specs=[anywhere] * 5,
        out_specs=(pl.BlockSpec(memory_space=pltpu.VMEM),) * 4,
        scratch_shapes=[
            vmem((2, 16, 32, 1280), bf),
            vmem((2560, 512), bf),
            vmem((8, 2, 160, 1280), bf),
            vmem((3, 16, 32, 1280), bf),
            vmem((16, 32, WIDE), bf),
            vmem((16, 32, WIDE), bf),
            vmem((2 * GROUP, 256, 256), f32),
            vmem((256, 256), f32),
            vmem((groups, 8, 160, WIDE), bf),
            vmem((groups, 8, 160, WIDE), bf),
            vmem((8, 160, WIDE), f32),
            vmem((groups, 8, 160, WIDE), bf),
            vmem((groups, 8, 160, WIDE), bf),
            vmem((8, 160, HS), bf),
            vmem((8, 160, HS), bf),
            vmem((8, 160, HS), bf),
            vmem((8, OWNED, 16, HS), bf),
            vmem((8, OWNED, 16, HS), bf),
            vmem((8, OWNED, 16, HS), bf),
            dma, dma((7,)), dma, dma, dma, dma, dma, dma, dma, dma, dma((groups,)), dma((groups,)),
            dma, dma, dma, dma((groups,)), dma((groups,)), dma((groups,)), dma((groups,)),
            dma, dma, dma, dma, dma, dma, dma, dma,
        ],
        compiler_params=pltpu.CompilerParams(
            collective_id=0, has_side_effects=True, vmem_limit_bytes=49 * 2**20
        ),
    )(query_heads, key_heads, value_heads, grad_out, out_weight)


def solution(mesh):
    placed = (
        P("dp", "tm", None, "mp"),
        P("dp", "tm", None, "mp"),
        P("dp", "tm", None, "mp"),
        P("dp", "tm", None, "mp"),
        P("dp", "mp"),
    )
    return jax.shard_map(
        on_device,
        mesh=mesh,
        in_specs=placed,
        out_specs=(
            P("dp", None, "tm", "mp"),
            P("dp", None, "tm", "mp"),
            P("dp", None, "tm", "mp"),
            P("dp", "mp"),
        ),
        check_vma=False,
    )
```

```python
import functools

import jax
import jax.numpy as jnp
from jax import lax
from jax.experimental import pallas as pl
from jax.experimental.pallas import tpu as pltpu
from jax.sharding import PartitionSpec as P

HS = 128
MESH = pl.DeviceIdType.MESH
AHEAD = 5
OWNED = 3


def kernel(
    heads, grad_scale, query, key, value, grad, weight,
    dq_out, dk_out, dv_out, GW,
    G, GT, W, QKV, DA, ATT, PR, BIAS, CSEND, CRECV, OWN, XSEND, XRECV, ASEND, ARECV, AALL, BSEND, BRECV, BALL,
    g_send, g_recv, gy_send, gy_recv, wh_send, wh_recv, w_send, w_recv, wf_send, wf_recv, q_send, q_recv,
    own_g, own_w, own_q, c_send, c_recv, x_send, x_recv, ar_send, ar_recv, ag_send, ag_recv, br_send, br_recv, bg_send, bg_recv,
):
    dp, z, m = lax.axis_index("dp"), lax.axis_index("tm"), lax.axis_index("mp")
    c, xh = lax.rem(dp, 2), dp // 2
    sibling = (dp + 1 - 2 * c, z, m)
    partner = (dp, z, 1 - m)

    def z_peer(d):
        return lax.rem(z + d, 8)

    def x_peer(d):
        return lax.rem(xh + d, 8)

    def drain(ref, sem):
        pltpu.make_async_copy(ref, ref, sem).wait()

    def remote(src, dst, ss, rs, to):
        pltpu.make_async_remote_copy(
            src_ref=src, dst_ref=dst, send_sem=ss, recv_sem=rs, device_id=to, device_id_type=MESH
        ).start()

    barrier = pltpu.get_barrier_semaphore()
    for to in [sibling, partner]:
        pl.semaphore_signal(barrier, inc=1, device_id=to, device_id_type=MESH)

    def greet(d, _):
        pl.semaphore_signal(barrier, inc=1, device_id=(dp, z_peer(d), m), device_id_type=MESH)
        pl.semaphore_signal(barrier, inc=1, device_id=(x_peer(d) * 2 + c, z, m), device_id_type=MESH)
        return 0

    lax.fori_loop(1, 8, greet, 0)
    mine = pl.ds(pl.multiple_of(z * 32, 32), 32)
    frames = pl.ds(2 * z, 2)
    pltpu.make_async_copy(grad.at[0, :, mine], G.at[m, frames], own_g).start()
    pltpu.make_async_copy(weight, W.at[xh, c], own_w).start()
    for a, src in enumerate((query, key, value)):
        pltpu.make_async_copy(src.at[0, :, mine], QKV.at[a, frames], own_q).start()
    pl.semaphore_wait(barrier, 16)

    order = (1, 7, 2, 6, 3, 5, 4)

    for i, d in enumerate(order):
        zz = z_peer(d)
        remote(
            grad.at[0, :, pl.ds(pl.multiple_of(zz * 32, 32), 32)], G.at[m, frames], g_send, g_recv.at[i], (dp, zz, m)
        )
    remote(grad.at[0, :, mine], G.at[m, frames], gy_send, gy_recv, partner)

    other = xh + 1 - 2 * lax.rem(xh, 2)
    remote(weight, W.at[xh, c], wh_send, wh_recv, (other * 2 + c, z, m))

    def send_w(src, slot):
        for d in (2, 6, 4):
            remote(src, W.at[slot, c], w_send, w_recv, (x_peer(d) * 2 + c, z, m))

    send_w(weight, xh)

    def columns(u, n):
        return pl.ds(pl.multiple_of(u * HS, HS), n * HS)

    def send_group(g, u, n):
        cols = columns(u, n)
        for d in order:
            zz = z_peer(d)
            rows = pl.ds(pl.multiple_of(zz * 32, 32), 32)
            for a, src in enumerate((query, key, value)):
                remote(
                    src.at[0, :, rows, cols], QKV.at[a, frames, :, cols], q_send.at[g], q_recv.at[g], (dp, zz, m)
                )

    send_group(0, 0, 1)
    send_group(1, 1, 1)
    row = lax.broadcasted_iota(jnp.int32, (256, 256), 0)
    col = lax.broadcasted_iota(jnp.int32, (256, 256), 1)
    BIAS[...] = jnp.where((lax.rem(row, 16) == lax.rem(col, 16)) & (col <= row), 0.0, -1e30).astype(jnp.float32)
    BSEND[...] = jnp.zeros(BSEND.shape, jnp.bfloat16)

    for i, d in enumerate(order):
        zz = lax.rem(z + 8 - d, 8)
        there = G.at[m, pl.ds(2 * zz, 2)]
        drain(there, g_recv.at[i])
        remote(there, there, gy_send, gy_recv, partner)
        if i == 1:
            drain(weight, wh_recv)
            send_w(W.at[other, c], other)

    def send_early(g, _):
        send_group(g, g, 1)
        return 0

    lax.fori_loop(2, AHEAD, send_early, 0)
    drain(grad.at[0, :, mine], own_g)

    def turn(half):
        def body(j, _):
            lanes = pl.ds(pl.multiple_of(j * 128, 128), 128)
            block = G[half, :, :, lanes].reshape(512, 128)
            GT[pl.ds(pl.multiple_of(half * 1280 + j * 128, 128), 128), :] = block.T
            return 0

        lax.fori_loop(0, 10, body, 0)

    turn(m)
    drain(W.at[pl.ds(0, 6), c], w_recv)
    drain(weight, own_w)
    remote(W.at[:, c], W.at[:, c], wf_send, wf_recv, sibling)
    drain(G.at[1 - m], gy_recv)
    turn(1 - m)
    drain(QKV.at[:, frames], own_q)

    def block_of(ref, b, lanes):
        return ref[:, pl.ds(16 * b, 16), lanes].reshape(256, HS)

    def rows_for(core):
        return jnp.concatenate(
            [GT[pl.ds(pl.multiple_of((2 * s + core) * 160, 32), 160), :] for s in range(8)], axis=0
        )

    def sum_xy(g, u, n):
        drain(XRECV.at[pl.ds(u, n), pl.ds(0, 7)], x_recv.at[g])
        for h in range(n):
            total = XSEND[u + h, xh].astype(jnp.float32)
            for d in range(1, 8):
                total = total + XRECV[u + h, x_peer(d)].astype(jnp.float32)
            yield h, total.astype(jnp.bfloat16)

    def scatter_z(src, dst, ss, rs):
        def send(d, _):
            zz = z_peer(d)
            remote(src.at[zz], dst.at[z], ss, rs, (dp, zz, m))
            return 0

        lax.fori_loop(1, 8, send, 0)

    def gather_z(src, dst, all_, rs, ss, gs):
        drain(dst.at[pl.ds(0, 7)], rs)
        total = src[z].astype(jnp.float32)
        for d in range(1, 8):
            total = total + dst[z_peer(d)].astype(jnp.float32)
        all_[z] = total.astype(jnp.bfloat16)

        def send(d, _):
            remote(all_.at[z], all_.at[z], ss, gs, (dp, z_peer(d), m))
            return 0

        lax.fori_loop(1, 8, send, 0)

    def head_rows(k):
        for _, part in sum_xy(k, k, 1):
            ASEND[k // 4, pl.ds(2 * lax.rem(k, 4), 2)] = part.reshape(2, 80, HS)

    def head_tiles(g, h):
        for _, part in sum_xy(g, 8 + h, 1):
            for t in range(10):
                at = 10 * h + t
                BSEND[at // OWNED, at % OWNED] = part[16 * t:16 * t + 16]

    def forward(u, n):
        for h in range(n):
            lanes = columns(u + h, 1)
            for b in range(2):
                q = block_of(QKV.at[0], b, lanes)
                kk = block_of(QKV.at[1], b, lanes)
                v = block_of(QKV.at[2], b, lanes)
                s = lax.dot_general(q, kk, (((1,), (1,)), ((), ())), preferred_element_type=jnp.float32)
                s = s * (HS ** -0.5) + BIAS[...]
                e = jnp.exp(s - jnp.max(s, axis=-1, keepdims=True))
                p = e / jnp.sum(e, axis=-1, keepdims=True)
                PR[2 * h + b] = p
                att = jnp.dot(p.astype(jnp.bfloat16), v, preferred_element_type=jnp.float32).astype(jnp.bfloat16)
                ATT[:, pl.ds(16 * b, 16), pl.ds(h * HS, HS)] = att.reshape(16, 16, HS)

    def sum_cores(g, u, n):
        att = ATT[:, :, :n * HS].reshape(512, n * HS)
        theirs = jnp.dot(rows_for(1 - c), att, preferred_element_type=jnp.float32).astype(jnp.bfloat16)
        for h in range(n):
            CSEND[u + h] = theirs[:, h * HS:(h + 1) * HS].reshape(8, 160, HS)
        part = pl.ds(u, n)
        remote(CSEND.at[part], CRECV.at[part], c_send.at[g], c_recv.at[g], sibling)
        own = jnp.dot(rows_for(c), att, preferred_element_type=jnp.float32)
        for h in range(n):
            OWN[h] = own[:, h * HS:(h + 1) * HS].reshape(8, 160, HS)

    def to_xy(g, u, n):
        part = pl.ds(u, n)
        drain(CRECV.at[part], c_recv.at[g])
        for h in range(n):
            for s in range(8):
                XSEND[u + h, s] = (OWN[h, s] + CRECV[u + h, s].astype(jnp.float32)).astype(jnp.bfloat16)

        def send(d, _):
            to = x_peer(d)
            remote(XSEND.at[part, to], XRECV.at[part, xh], x_send.at[g], x_recv.at[g], (to * 2 + c, z, m))
            return 0

        lax.fori_loop(1, 8, send, 0)

    def d_attended(u, n):
        cols = columns(u, n)
        low = W[pl.ds(0, 4), :, :, cols].reshape(1280, n * HS)
        high = W[pl.ds(4, 4), :, :, cols].reshape(1280, n * HS)
        da = jnp.dot(G[0].reshape(512, 1280), low, preferred_element_type=jnp.float32)
        da = da + jnp.dot(G[1].reshape(512, 1280), high, preferred_element_type=jnp.float32)
        DA[:, :, :n * HS] = da.astype(jnp.bfloat16).reshape(16, 32, n * HS)

    def backward(u, n):
        for h in range(n):
            lanes = columns(u + h, 1)
            for b in range(2):
                q = block_of(QKV.at[0], b, lanes)
                kk = block_of(QKV.at[1], b, lanes)
                v = block_of(QKV.at[2], b, lanes)
                d_att = block_of(DA, b, pl.ds(h * HS, HS))
                p = PR[2 * h + b]
                dp_ = lax.dot_general(d_att, v, (((1,), (1,)), ((), ())), preferred_element_type=jnp.float32)
                inner = jnp.sum(p * dp_, axis=-1, keepdims=True)
                ds = (p * (dp_ - inner)).astype(jnp.bfloat16)
                over_rows = (((0,), (0,)), ((), ()))
                dq = jnp.dot(ds, kk, preferred_element_type=jnp.float32) * (HS ** -0.5)
                dk = lax.dot_general(ds, q, over_rows, preferred_element_type=jnp.float32) * (HS ** -0.5)
                dv = lax.dot_general(p.astype(jnp.bfloat16), d_att, over_rows, preferred_element_type=jnp.float32)
                for dst, r in ((dq_out, dq), (dk_out, dk), (dv_out, dv)):
                    dst[0, :, pl.ds(16 * b, 16), lanes] = r.astype(jnp.bfloat16).reshape(16, 16, HS)

    def one(k, _):
        @pl.when(k >= 2)
        def _():
            head_rows(k - 2)

        drain(QKV.at[:, pl.ds(0, 14), :, columns(k, 1)], q_recv.at[k])

        @pl.when(k == heads - 1)
        def _():
            for i in range(2):
                scatter_z(ASEND.at[i], ARECV.at[i], ar_send.at[i], ar_recv.at[i])

        @pl.when(k + AHEAD < heads)
        def _():
            send_group(k + AHEAD, k + AHEAD, 1)

        forward(k, 1)
        sum_cores(k, k, 1)
        to_xy(k, k, 1)

        @pl.when(k == 0)
        def _():
            drain(W.at[:, 1 - c], wf_recv)

        d_attended(k, 1)
        backward(k, 1)
        return 0

    lax.fori_loop(0, heads, one, 0)
    head_tiles(heads - 2, 0)

    def gather_rows(i):
        gather_z(ASEND.at[i], ARECV.at[i], AALL.at[i], ar_recv.at[i], ag_send.at[i], ag_recv.at[i])

    gather_rows(0)
    head_tiles(heads - 1, 1)
    scatter_z(BSEND, BRECV, br_send, br_recv)
    gather_rows(1)
    gather_z(BSEND, BRECV, BALL, br_recv, bg_send, bg_recv)
    for i in range(2):
        drain(AALL.at[i, pl.ds(0, 7)], ag_recv.at[i])
        for u in range(4):
            rows = AALL[i, 2 * u:2 * u + 2].astype(jnp.float32).reshape(160, HS)
            GW[:, (4 * i + u) * HS:(4 * i + u + 1) * HS] = rows * grad_scale
    drain(BALL.at[pl.ds(0, 7)], bg_recv)
    for h in range(2):
        for t in range(10):
            at = 10 * h + t
            lanes = pl.ds((8 + h) * HS, HS)
            GW[16 * t:16 * t + 16, lanes] = BALL[at // OWNED, at % OWNED].astype(jnp.float32) * grad_scale

    drain(G.at[m, pl.ds(0, 14)], g_send)
    drain(G.at[m], gy_send)
    drain(weight, wh_send)
    drain(W.at[pl.ds(0, 6), c], w_send)
    drain(W.at[:, c], wf_send)

    def settle(g, _):
        u, n = g, 1
        drain(QKV.at[:, pl.ds(0, 14), :, columns(u, n)], q_send.at[g])
        drain(CSEND.at[pl.ds(u, n)], c_send.at[g])
        drain(XSEND.at[pl.ds(u, n), pl.ds(0, 7)], x_send.at[g])
        return 0

    lax.fori_loop(0, heads, settle, 0)
    for i in range(2):
        drain(ARECV.at[i, pl.ds(0, 7)], ar_send.at[i])
        drain(ARECV.at[i, pl.ds(0, 7)], ag_send.at[i])
    drain(BRECV.at[pl.ds(0, 7)], br_send)
    drain(BRECV.at[pl.ds(0, 7)], bg_send)


def hand_on(*refs):
    sems = refs[8]
    copies = [pltpu.make_async_copy(s, d, sems.at[i]) for i, (s, d) in enumerate(zip(refs[:4], refs[4:8]))]
    for copy in copies:
        copy.start()
    for copy in copies:
        copy.wait()


def on_device(query_heads, key_heads, value_heads, grad_out, out_weight):
    heads = query_heads.shape[3] // HS
    groups = heads
    bf, f32 = jnp.bfloat16, jnp.float32
    dma, vmem = pltpu.SemaphoreType.DMA, pltpu.VMEM
    anywhere = pl.BlockSpec(memory_space=pltpu.HBM)
    part = jax.ShapeDtypeStruct((1, 16, 32, 1280), bf)
    results = pl.pallas_call(
        functools.partial(kernel, heads, float(16 * 16 * 256) ** -0.5),
        out_shape=(part, part, part, jax.ShapeDtypeStruct((160, 1280), f32)),
        in_specs=[anywhere] * 5,
        out_specs=(pl.BlockSpec(memory_space=pltpu.VMEM),) * 4,
        scratch_shapes=[
            vmem((2, 16, 32, 1280), bf),
            vmem((2560, 512), bf),
            vmem((8, 2, 160, 1280), bf),
            vmem((3, 16, 32, 1280), bf),
            vmem((16, 32, HS), bf),
            vmem((16, 32, HS), bf),
            vmem((2, 256, 256), f32),
            vmem((256, 256), f32),
            vmem((heads, 8, 160, HS), bf),
            vmem((heads, 8, 160, HS), bf),
            vmem((1, 8, 160, HS), f32),
            vmem((heads, 8, 160, HS), bf),
            vmem((heads, 8, 160, HS), bf),
            vmem((2, 8, 80, HS), bf),
            vmem((2, 8, 80, HS), bf),
            vmem((2, 8, 80, HS), bf),
            vmem((8, OWNED, 16, HS), bf),
            vmem((8, OWNED, 16, HS), bf),
            vmem((8, OWNED, 16, HS), bf),
            dma, dma((7,)), dma, dma, dma, dma, dma, dma, dma, dma, dma((groups,)), dma((groups,)),
            dma, dma, dma, dma((groups,)), dma((groups,)), dma((groups,)), dma((groups,)),
            dma((2,)), dma((2,)), dma((2,)), dma((2,)), dma, dma, dma, dma,
        ],
        compiler_params=pltpu.CompilerParams(
            collective_id=0, has_side_effects=True, vmem_limit_bytes=49 * 2**20
        ),
    )(query_heads, key_heads, value_heads, grad_out, out_weight)
    return pl.pallas_call(
        hand_on,
        out_shape=(part, part, part, jax.ShapeDtypeStruct((160, 1280), f32)),
        in_specs=[pl.BlockSpec(memory_space=pl.ANY)] * 4,
        out_specs=(anywhere,) * 4,
        scratch_shapes=[dma((4,))],
        compiler_params=pltpu.CompilerParams(vmem_limit_bytes=2**20),
    )(*results)


def solution(mesh):
    placed = (
        P("dp", "tm", None, "mp"),
        P("dp", "tm", None, "mp"),
        P("dp", "tm", None, "mp"),
        P("dp", "tm", None, "mp"),
        P("dp", "mp"),
    )
    return jax.shard_map(
        on_device,
        mesh=mesh,
        in_specs=placed,
        out_specs=(
            P("dp", None, "tm", "mp"),
            P("dp", None, "tm", "mp"),
            P("dp", None, "tm", "mp"),
            P("dp", "mp"),
        ),
        check_vma=False,
    )
```

```python
import functools

import jax
import jax.numpy as jnp
from jax import lax
from jax.experimental import pallas as pl
from jax.experimental.pallas import tpu as pltpu
from jax.sharding import PartitionSpec as P

HS = 128
MESH = pl.DeviceIdType.MESH
AHEAD = 5
OWNED = 3


def kernel(
    heads, grad_scale, query, key, value, grad, weight,
    dq_out, dk_out, dv_out, GW,
    G, GT, W, QKV, DA, ATT, PR, BIAS, CSEND, CRECV, OWN, XSEND, XRECV, ASEND, ARECV, AALL, BSEND, BRECV, BALL,
    g_send, g_recv, gy_send, gy_recv, wh_send, wh_recv, w_send, w_recv, wf_send, wf_recv, q_send, q_recv,
    own_g, own_w, own_q, c_send, c_recv, x_send, x_recv, ar_send, ar_recv, ag_send, ag_recv, br_send, br_recv, bg_send, bg_recv,
):
    dp, z, m = lax.axis_index("dp"), lax.axis_index("tm"), lax.axis_index("mp")
    c, xh = lax.rem(dp, 2), dp // 2
    sibling = (dp + 1 - 2 * c, z, m)
    partner = (dp, z, 1 - m)

    def z_peer(d):
        return lax.rem(z + d, 8)

    def x_peer(d):
        return lax.rem(xh + d, 8)

    def far_first(i):
        return 4 + ((i + 1) // 2) * (1 - 2 * lax.rem(i, 2))

    def drain(ref, sem):
        pltpu.make_async_copy(ref, ref, sem).wait()

    def remote(src, dst, ss, rs, to):
        pltpu.make_async_remote_copy(
            src_ref=src, dst_ref=dst, send_sem=ss, recv_sem=rs, device_id=to, device_id_type=MESH
        ).start()

    barrier = pltpu.get_barrier_semaphore()
    for to in [sibling, partner]:
        pl.semaphore_signal(barrier, inc=1, device_id=to, device_id_type=MESH)

    def greet(d, _):
        pl.semaphore_signal(barrier, inc=1, device_id=(dp, z_peer(d), m), device_id_type=MESH)
        pl.semaphore_signal(barrier, inc=1, device_id=(x_peer(d) * 2 + c, z, m), device_id_type=MESH)
        return 0

    lax.fori_loop(1, 8, greet, 0)
    mine = pl.ds(pl.multiple_of(z * 32, 32), 32)
    frames = pl.ds(2 * z, 2)
    pltpu.make_async_copy(grad.at[0, :, mine], G.at[m, frames], own_g).start()
    pltpu.make_async_copy(weight, W.at[xh, c], own_w).start()
    for a, src in enumerate((query, key, value)):
        pltpu.make_async_copy(src.at[0, :, mine], QKV.at[a, frames], own_q).start()
    pl.semaphore_wait(barrier, 16)

    order = (4, 3, 5, 2, 6, 1, 7)

    for i, d in enumerate(order):
        zz = z_peer(d)
        remote(
            grad.at[0, :, pl.ds(pl.multiple_of(zz * 32, 32), 32)], G.at[m, frames], g_send, g_recv.at[i], (dp, zz, m)
        )
    remote(grad.at[0, :, mine], G.at[m, frames], gy_send, gy_recv, partner)

    other = xh + 1 - 2 * lax.rem(xh, 2)
    remote(weight, W.at[xh, c], wh_send, wh_recv, (other * 2 + c, z, m))

    def send_w(src, slot):
        for d in (2, 6, 4):
            remote(src, W.at[slot, c], w_send, w_recv, (x_peer(d) * 2 + c, z, m))

    send_w(weight, xh)

    def columns(u, n):
        return pl.ds(pl.multiple_of(u * HS, HS), n * HS)

    def send_group(g, u, n):
        cols = columns(u, n)
        for d in order:
            zz = z_peer(d)
            rows = pl.ds(pl.multiple_of(zz * 32, 32), 32)
            for a, src in enumerate((query, key, value)):
                remote(
                    src.at[0, :, rows, cols], QKV.at[a, frames, :, cols], q_send.at[g], q_recv.at[g], (dp, zz, m)
                )

    send_group(0, 0, 1)
    send_group(1, 1, 1)
    row = lax.broadcasted_iota(jnp.int32, (256, 256), 0)
    col = lax.broadcasted_iota(jnp.int32, (256, 256), 1)
    BIAS[...] = jnp.where((lax.rem(row, 16) == lax.rem(col, 16)) & (col <= row), 0.0, -1e30).astype(jnp.float32)
    BSEND[...] = jnp.zeros(BSEND.shape, jnp.bfloat16)

    for i, d in enumerate(order):
        zz = lax.rem(z + 8 - d, 8)
        there = G.at[m, pl.ds(2 * zz, 2)]
        drain(there, g_recv.at[i])
        remote(there, there, gy_send, gy_recv, partner)
        if i == 1:
            drain(weight, wh_recv)
            send_w(W.at[other, c], other)

    def send_early(g, _):
        send_group(g, g, 1)
        return 0

    lax.fori_loop(2, AHEAD, send_early, 0)
    drain(grad.at[0, :, mine], own_g)

    def turn(half):
        def body(j, _):
            lanes = pl.ds(pl.multiple_of(j * 128, 128), 128)
            block = G[half, :, :, lanes].reshape(512, 128)
            GT[pl.ds(pl.multiple_of(half * 1280 + j * 128, 128), 128), :] = block.T
            return 0

        lax.fori_loop(0, 10, body, 0)

    turn(m)
    drain(W.at[pl.ds(0, 6), c], w_recv)
    drain(weight, own_w)
    remote(W.at[:, c], W.at[:, c], wf_send, wf_recv, sibling)
    drain(G.at[1 - m], gy_recv)
    turn(1 - m)
    drain(QKV.at[:, frames], own_q)

    def block_of(ref, b, lanes):
        return ref[:, pl.ds(16 * b, 16), lanes].reshape(256, HS)

    def rows_for(core):
        return jnp.concatenate(
            [GT[pl.ds(pl.multiple_of((2 * s + core) * 160, 32), 160), :] for s in range(8)], axis=0
        )

    def sum_xy(g, u, n):
        drain(XRECV.at[pl.ds(u, n), pl.ds(0, 7)], x_recv.at[g])
        for h in range(n):
            total = XSEND[u + h, xh].astype(jnp.float32)
            for d in range(1, 8):
                total = total + XRECV[u + h, x_peer(d)].astype(jnp.float32)
            yield h, total.astype(jnp.bfloat16)

    def scatter_z(src, dst, ss, rs):
        def send(i, _):
            zz = z_peer(far_first(i))
            remote(src.at[zz], dst.at[z], ss, rs, (dp, zz, m))
            return 0

        lax.fori_loop(0, 7, send, 0)

    def gather_z(src, dst, all_, rs, ss, gs):
        drain(dst.at[pl.ds(0, 7)], rs)
        total = src[z].astype(jnp.float32)
        for d in range(1, 8):
            total = total + dst[z_peer(d)].astype(jnp.float32)
        all_[z] = total.astype(jnp.bfloat16)

        def send(i, _):
            remote(all_.at[z], all_.at[z], ss, gs, (dp, z_peer(far_first(i)), m))
            return 0

        lax.fori_loop(0, 7, send, 0)

    def head_rows(k):
        for _, part in sum_xy(k, k, 1):
            ASEND[k // 4, pl.ds(2 * lax.rem(k, 4), 2)] = part.reshape(2, 80, HS)

    def head_tiles(g, h):
        for _, part in sum_xy(g, 8 + h, 1):
            for t in range(10):
                at = 10 * h + t
                BSEND[at // OWNED, at % OWNED] = part[16 * t:16 * t + 16]

    def forward(u, n):
        for h in range(n):
            lanes = columns(u + h, 1)
            for b in range(2):
                q = block_of(QKV.at[0], b, lanes)
                kk = block_of(QKV.at[1], b, lanes)
                v = block_of(QKV.at[2], b, lanes)
                s = lax.dot_general(q, kk, (((1,), (1,)), ((), ())), preferred_element_type=jnp.float32)
                s = s * (HS ** -0.5) + BIAS[...]
                e = jnp.exp(s - jnp.max(s, axis=-1, keepdims=True))
                p = e / jnp.sum(e, axis=-1, keepdims=True)
                PR[2 * h + b] = p
                att = jnp.dot(p.astype(jnp.bfloat16), v, preferred_element_type=jnp.float32).astype(jnp.bfloat16)
                ATT[:, pl.ds(16 * b, 16), pl.ds(h * HS, HS)] = att.reshape(16, 16, HS)

    def sum_cores(g, u, n):
        att = ATT[:, :, :n * HS].reshape(512, n * HS)
        theirs = jnp.dot(rows_for(1 - c), att, preferred_element_type=jnp.float32).astype(jnp.bfloat16)
        for h in range(n):
            CSEND[u + h] = theirs[:, h * HS:(h + 1) * HS].reshape(8, 160, HS)
        part = pl.ds(u, n)
        remote(CSEND.at[part], CRECV.at[part], c_send.at[g], c_recv.at[g], sibling)
        own = jnp.dot(rows_for(c), att, preferred_element_type=jnp.float32)
        for h in range(n):
            OWN[h] = own[:, h * HS:(h + 1) * HS].reshape(8, 160, HS)

    def to_xy(g, u, n):
        part = pl.ds(u, n)
        drain(CRECV.at[part], c_recv.at[g])
        for h in range(n):
            for s in range(8):
                XSEND[u + h, s] = (OWN[h, s] + CRECV[u + h, s].astype(jnp.float32)).astype(jnp.bfloat16)

        def send(i, _):
            to = x_peer(far_first(i))
            remote(XSEND.at[part, to], XRECV.at[part, xh], x_send.at[g], x_recv.at[g], (to * 2 + c, z, m))
            return 0

        lax.fori_loop(0, 7, send, 0)

    def d_attended(u, n):
        cols = columns(u, n)
        low = W[pl.ds(0, 4), :, :, cols].reshape(1280, n * HS)
        high = W[pl.ds(4, 4), :, :, cols].reshape(1280, n * HS)
        da = jnp.dot(G[0].reshape(512, 1280), low, preferred_element_type=jnp.float32)
        da = da + jnp.dot(G[1].reshape(512, 1280), high, preferred_element_type=jnp.float32)
        DA[:, :, :n * HS] = da.astype(jnp.bfloat16).reshape(16, 32, n * HS)

    def backward(u, n):
        for h in range(n):
            lanes = columns(u + h, 1)
            for b in range(2):
                q = block_of(QKV.at[0], b, lanes)
                kk = block_of(QKV.at[1], b, lanes)
                v = block_of(QKV.at[2], b, lanes)
                d_att = block_of(DA, b, pl.ds(h * HS, HS))
                p = PR[2 * h + b]
                dp_ = lax.dot_general(d_att, v, (((1,), (1,)), ((), ())), preferred_element_type=jnp.float32)
                inner = jnp.sum(p * dp_, axis=-1, keepdims=True)
                ds = (p * (dp_ - inner)).astype(jnp.bfloat16)
                over_rows = (((0,), (0,)), ((), ()))
                dq = jnp.dot(ds, kk, preferred_element_type=jnp.float32) * (HS ** -0.5)
                dk = lax.dot_general(ds, q, over_rows, preferred_element_type=jnp.float32) * (HS ** -0.5)
                dv = lax.dot_general(p.astype(jnp.bfloat16), d_att, over_rows, preferred_element_type=jnp.float32)
                for dst, r in ((dq_out, dq), (dk_out, dk), (dv_out, dv)):
                    dst[0, :, pl.ds(16 * b, 16), lanes] = r.astype(jnp.bfloat16).reshape(16, 16, HS)

    def one(k, _):
        @pl.when(k >= 2)
        def _():
            head_rows(k - 2)

        drain(QKV.at[:, pl.ds(0, 14), :, columns(k, 1)], q_recv.at[k])

        @pl.when(k == heads - 1)
        def _():
            for i in range(2):
                scatter_z(ASEND.at[i], ARECV.at[i], ar_send.at[i], ar_recv.at[i])

        @pl.when(k + AHEAD < heads)
        def _():
            send_group(k + AHEAD, k + AHEAD, 1)

        forward(k, 1)
        sum_cores(k, k, 1)
        to_xy(k, k, 1)

        @pl.when(k == 0)
        def _():
            drain(W.at[:, 1 - c], wf_recv)

        d_attended(k, 1)
        backward(k, 1)
        return 0

    lax.fori_loop(0, heads, one, 0)
    head_tiles(heads - 2, 0)

    def gather_rows(i):
        gather_z(ASEND.at[i], ARECV.at[i], AALL.at[i], ar_recv.at[i], ag_send.at[i], ag_recv.at[i])

    gather_rows(0)
    head_tiles(heads - 1, 1)
    scatter_z(BSEND, BRECV, br_send, br_recv)
    gather_rows(1)
    gather_z(BSEND, BRECV, BALL, br_recv, bg_send, bg_recv)
    for i in range(2):
        drain(AALL.at[i, pl.ds(0, 7)], ag_recv.at[i])
        for u in range(4):
            rows = AALL[i, 2 * u:2 * u + 2].astype(jnp.float32).reshape(160, HS)
            GW[:, (4 * i + u) * HS:(4 * i + u + 1) * HS] = rows * grad_scale
    drain(BALL.at[pl.ds(0, 7)], bg_recv)
    for h in range(2):
        for t in range(10):
            at = 10 * h + t
            lanes = pl.ds((8 + h) * HS, HS)
            GW[16 * t:16 * t + 16, lanes] = BALL[at // OWNED, at % OWNED].astype(jnp.float32) * grad_scale

    drain(G.at[m, pl.ds(0, 14)], g_send)
    drain(G.at[m], gy_send)
    drain(weight, wh_send)
    drain(W.at[pl.ds(0, 6), c], w_send)
    drain(W.at[:, c], wf_send)

    def settle(g, _):
        u, n = g, 1
        drain(QKV.at[:, pl.ds(0, 14), :, columns(u, n)], q_send.at[g])
        drain(CSEND.at[pl.ds(u, n)], c_send.at[g])
        drain(XSEND.at[pl.ds(u, n), pl.ds(0, 7)], x_send.at[g])
        return 0

    lax.fori_loop(0, heads, settle, 0)
    for i in range(2):
        drain(ARECV.at[i, pl.ds(0, 7)], ar_send.at[i])
        drain(ARECV.at[i, pl.ds(0, 7)], ag_send.at[i])
    drain(BRECV.at[pl.ds(0, 7)], br_send)
    drain(BRECV.at[pl.ds(0, 7)], bg_send)


def hand_on(*refs):
    sems = refs[8]
    copies = [
        pltpu.make_async_copy(s.at[0, pl.ds(8 * i, 8)], d.at[0, pl.ds(8 * i, 8)], sems.at[a, i])
        for a, (s, d) in enumerate(zip(refs[:3], refs[4:7]))
        for i in range(2)
    ]
    copies.append(pltpu.make_async_copy(refs[3], refs[7], sems.at[3, 0]))
    for copy in copies:
        copy.start()
    for copy in copies:
        copy.wait()


def on_device(query_heads, key_heads, value_heads, grad_out, out_weight):
    heads = query_heads.shape[3] // HS
    groups = heads
    bf, f32 = jnp.bfloat16, jnp.float32
    dma, vmem = pltpu.SemaphoreType.DMA, pltpu.VMEM
    anywhere = pl.BlockSpec(memory_space=pltpu.HBM)
    part = jax.ShapeDtypeStruct((1, 16, 32, 1280), bf)
    results = pl.pallas_call(
        functools.partial(kernel, heads, float(16 * 16 * 256) ** -0.5),
        out_shape=(part, part, part, jax.ShapeDtypeStruct((160, 1280), f32)),
        in_specs=[anywhere] * 5,
        out_specs=(pl.BlockSpec(memory_space=pltpu.VMEM),) * 4,
        scratch_shapes=[
            vmem((2, 16, 32, 1280), bf),
            vmem((2560, 512), bf),
            vmem((8, 2, 160, 1280), bf),
            vmem((3, 16, 32, 1280), bf),
            vmem((16, 32, HS), bf),
            vmem((16, 32, HS), bf),
            vmem((2, 256, 256), f32),
            vmem((256, 256), f32),
            vmem((heads, 8, 160, HS), bf),
            vmem((heads, 8, 160, HS), bf),
            vmem((1, 8, 160, HS), f32),
            vmem((heads, 8, 160, HS), bf),
            vmem((heads, 8, 160, HS), bf),
            vmem((2, 8, 80, HS), bf),
            vmem((2, 8, 80, HS), bf),
            vmem((2, 8, 80, HS), bf),
            vmem((8, OWNED, 16, HS), bf),
            vmem((8, OWNED, 16, HS), bf),
            vmem((8, OWNED, 16, HS), bf),
            dma, dma((7,)), dma, dma, dma, dma, dma, dma, dma, dma, dma((groups,)), dma((groups,)),
            dma, dma, dma, dma((groups,)), dma((groups,)), dma((groups,)), dma((groups,)),
            dma((2,)), dma((2,)), dma((2,)), dma((2,)), dma, dma, dma, dma,
        ],
        compiler_params=pltpu.CompilerParams(
            collective_id=0, has_side_effects=True, vmem_limit_bytes=49 * 2**20
        ),
    )(query_heads, key_heads, value_heads, grad_out, out_weight)
    return pl.pallas_call(
        hand_on,
        out_shape=(part, part, part, jax.ShapeDtypeStruct((160, 1280), f32)),
        in_specs=[pl.BlockSpec(memory_space=pl.ANY)] * 4,
        out_specs=(anywhere,) * 4,
        scratch_shapes=[dma((4, 2))],
        compiler_params=pltpu.CompilerParams(vmem_limit_bytes=2**20),
    )(*results)


def solution(mesh):
    placed = (
        P("dp", "tm", None, "mp"),
        P("dp", "tm", None, "mp"),
        P("dp", "tm", None, "mp"),
        P("dp", "tm", None, "mp"),
        P("dp", "mp"),
    )
    return jax.shard_map(
        on_device,
        mesh=mesh,
        in_specs=placed,
        out_specs=(
            P("dp", None, "tm", "mp"),
            P("dp", None, "tm", "mp"),
            P("dp", None, "tm", "mp"),
            P("dp", "mp"),
        ),
        check_vma=False,
    )
```

```python
import functools

import jax
import jax.numpy as jnp
from jax import lax
from jax.experimental import pallas as pl
from jax.experimental.pallas import tpu as pltpu
from jax.sharding import PartitionSpec as P

HS = 128
MESH = pl.DeviceIdType.MESH
AHEAD = 5
OWNED = 3


def kernel(
    heads, grad_scale, query, key, value, grad, weight,
    dq_out, dk_out, dv_out, GW,
    G, GT, W, QKV, DA, ATT, PR, BIAS, CSEND, CRECV, OWN, XSEND, XRECV, ASEND, ARECV, AALL, BSEND, BRECV, BALL,
    g_send, g_recv, gy_send, gy_recv, wh_send, wh_recv, w_send, w_recv, wf_send, wf_recv, q_send, q_recv,
    own_g, own_w, own_q, c_send, c_recv, x_send, x_recv, ar_send, ar_recv, ag_send, ag_recv, br_send, br_recv, bg_send, bg_recv,
):
    dp, z, m = lax.axis_index("dp"), lax.axis_index("tm"), lax.axis_index("mp")
    c, xh = lax.rem(dp, 2), dp // 2
    sibling = (dp + 1 - 2 * c, z, m)
    partner = (dp, z, 1 - m)

    def z_peer(d):
        return lax.rem(z + d, 8)

    def x_peer(d):
        return lax.rem(xh + d, 8)

    def far_first(i):
        return 4 + ((i + 1) // 2) * (1 - 2 * lax.rem(i, 2))

    def drain(ref, sem):
        pltpu.make_async_copy(ref, ref, sem).wait()

    def remote(src, dst, ss, rs, to):
        pltpu.make_async_remote_copy(
            src_ref=src, dst_ref=dst, send_sem=ss, recv_sem=rs, device_id=to, device_id_type=MESH
        ).start()

    barrier = pltpu.get_barrier_semaphore()
    for to in [sibling, partner]:
        pl.semaphore_signal(barrier, inc=1, device_id=to, device_id_type=MESH)

    def greet(d, _):
        pl.semaphore_signal(barrier, inc=1, device_id=(dp, z_peer(d), m), device_id_type=MESH)
        pl.semaphore_signal(barrier, inc=1, device_id=(x_peer(d) * 2 + c, z, m), device_id_type=MESH)
        return 0

    lax.fori_loop(1, 8, greet, 0)
    mine = pl.ds(pl.multiple_of(z * 32, 32), 32)
    frames = pl.ds(2 * z, 2)
    pltpu.make_async_copy(grad.at[0, :, mine], G.at[m, frames], own_g).start()
    pltpu.make_async_copy(weight, W.at[xh, c], own_w).start()
    for a, src in enumerate((query, key, value)):
        pltpu.make_async_copy(src.at[0, :, mine], QKV.at[a, frames], own_q).start()
    pl.semaphore_wait(barrier, 16)

    order = (4, 3, 5, 2, 6, 1, 7)

    for i, d in enumerate(order):
        zz = z_peer(d)
        remote(
            grad.at[0, :, pl.ds(pl.multiple_of(zz * 32, 32), 32)], G.at[m, frames], g_send, g_recv.at[i], (dp, zz, m)
        )
    remote(grad.at[0, :, mine], G.at[m, frames], gy_send, gy_recv, partner)

    other = xh + 1 - 2 * lax.rem(xh, 2)
    remote(weight, W.at[xh, c], wh_send, wh_recv, (other * 2 + c, z, m))

    def send_w(src, slot):
        for d in (2, 6, 4):
            remote(src, W.at[slot, c], w_send, w_recv, (x_peer(d) * 2 + c, z, m))

    send_w(weight, xh)

    def columns(u, n):
        return pl.ds(pl.multiple_of(u * HS, HS), n * HS)

    def send_group(g, u, n):
        cols = columns(u, n)
        for d in order:
            zz = z_peer(d)
            rows = pl.ds(pl.multiple_of(zz * 32, 32), 32)
            for a, src in enumerate((query, key, value)):
                remote(
                    src.at[0, :, rows, cols], QKV.at[a, frames, :, cols], q_send.at[g], q_recv.at[g], (dp, zz, m)
                )

    send_group(0, 0, 1)
    send_group(1, 1, 1)
    row = lax.broadcasted_iota(jnp.int32, (256, 256), 0)
    col = lax.broadcasted_iota(jnp.int32, (256, 256), 1)
    BIAS[...] = jnp.where((lax.rem(row, 16) == lax.rem(col, 16)) & (col <= row), 0.0, -1e30).astype(jnp.float32)
    BSEND[...] = jnp.zeros(BSEND.shape, jnp.bfloat16)

    for i, d in enumerate(order):
        zz = lax.rem(z + 8 - d, 8)
        there = G.at[m, pl.ds(2 * zz, 2)]
        drain(there, g_recv.at[i])
        remote(there, there, gy_send, gy_recv, partner)
        if i == 1:
            drain(weight, wh_recv)
            send_w(W.at[other, c], other)

    def send_early(g, _):
        send_group(g, g, 1)
        return 0

    lax.fori_loop(2, AHEAD, send_early, 0)
    drain(grad.at[0, :, mine], own_g)

    def turn(half):
        def body(j, _):
            lanes = pl.ds(pl.multiple_of(j * 128, 128), 128)
            block = G[half, :, :, lanes].reshape(512, 128)
            GT[pl.ds(pl.multiple_of(half * 1280 + j * 128, 128), 128), :] = block.T
            return 0

        lax.fori_loop(0, 10, body, 0)

    turn(m)
    drain(W.at[pl.ds(0, 6), c], w_recv)
    drain(weight, own_w)
    remote(W.at[:, c], W.at[:, c], wf_send, wf_recv, sibling)
    drain(G.at[1 - m], gy_recv)
    turn(1 - m)
    drain(QKV.at[:, frames], own_q)

    def block_of(ref, b, lanes):
        return ref[:, pl.ds(16 * b, 16), lanes].reshape(256, HS)

    def rows_for(core):
        return jnp.concatenate(
            [GT[pl.ds(pl.multiple_of((2 * s + core) * 160, 32), 160), :] for s in range(8)], axis=0
        )

    def sum_xy(g, u, n):
        drain(XRECV.at[pl.ds(u, n), pl.ds(0, 7)], x_recv.at[g])
        for h in range(n):
            total = XSEND[u + h, xh].astype(jnp.float32)
            for d in range(1, 8):
                total = total + XRECV[u + h, x_peer(d)].astype(jnp.float32)
            yield h, total.astype(jnp.bfloat16)

    def scatter_z(src, dst, ss, rs):
        def send(i, _):
            zz = z_peer(far_first(i))
            remote(src.at[zz], dst.at[z], ss, rs, (dp, zz, m))
            return 0

        lax.fori_loop(0, 7, send, 0)

    def gather_z(src, dst, all_, rs, ss, gs):
        drain(dst.at[pl.ds(0, 7)], rs)
        total = src[z].astype(jnp.float32)
        for d in range(1, 8):
            total = total + dst[z_peer(d)].astype(jnp.float32)
        all_[z] = total.astype(jnp.bfloat16)

        def send(i, _):
            remote(all_.at[z], all_.at[z], ss, gs, (dp, z_peer(far_first(i)), m))
            return 0

        lax.fori_loop(0, 7, send, 0)

    def head_rows(k):
        for _, part in sum_xy(k, k, 1):
            ASEND[k // 4, pl.ds(2 * lax.rem(k, 4), 2)] = part.reshape(2, 80, HS)

    def head_tiles(g, h):
        for _, part in sum_xy(g, 8 + h, 1):
            for t in range(10):
                at = 10 * h + t
                BSEND[at // OWNED, at % OWNED] = part[16 * t:16 * t + 16]

    def forward(u, n):
        for h in range(n):
            lanes = columns(u + h, 1)
            for b in range(2):
                q = block_of(QKV.at[0], b, lanes)
                kk = block_of(QKV.at[1], b, lanes)
                v = block_of(QKV.at[2], b, lanes)
                s = lax.dot_general(q, kk, (((1,), (1,)), ((), ())), preferred_element_type=jnp.float32)
                s = s * (HS ** -0.5) + BIAS[...]
                e = jnp.exp(s - jnp.max(s, axis=-1, keepdims=True))
                p = e / jnp.sum(e, axis=-1, keepdims=True)
                PR[2 * h + b] = p
                att = jnp.dot(p.astype(jnp.bfloat16), v, preferred_element_type=jnp.float32).astype(jnp.bfloat16)
                ATT[:, pl.ds(16 * b, 16), pl.ds(h * HS, HS)] = att.reshape(16, 16, HS)

    def sum_cores(g, u, n):
        att = ATT[:, :, :n * HS].reshape(512, n * HS)
        theirs = jnp.dot(rows_for(1 - c), att, preferred_element_type=jnp.float32).astype(jnp.bfloat16)
        for h in range(n):
            CSEND[u + h] = theirs[:, h * HS:(h + 1) * HS].reshape(8, 160, HS)
        part = pl.ds(u, n)
        remote(CSEND.at[part], CRECV.at[part], c_send.at[g], c_recv.at[g], sibling)
        own = jnp.dot(rows_for(c), att, preferred_element_type=jnp.float32)
        for h in range(n):
            OWN[h] = own[:, h * HS:(h + 1) * HS].reshape(8, 160, HS)

    def to_xy(g, u, n):
        part = pl.ds(u, n)
        drain(CRECV.at[part], c_recv.at[g])
        for h in range(n):
            for s in range(8):
                XSEND[u + h, s] = (OWN[h, s] + CRECV[u + h, s].astype(jnp.float32)).astype(jnp.bfloat16)

        def send(i, _):
            to = x_peer(far_first(i))
            remote(XSEND.at[part, to], XRECV.at[part, xh], x_send.at[g], x_recv.at[g], (to * 2 + c, z, m))
            return 0

        lax.fori_loop(0, 7, send, 0)

    def d_attended(u, n):
        cols = columns(u, n)
        low = W[pl.ds(0, 4), :, :, cols].reshape(1280, n * HS)
        high = W[pl.ds(4, 4), :, :, cols].reshape(1280, n * HS)
        da = jnp.dot(G[0].reshape(512, 1280), low, preferred_element_type=jnp.float32)
        da = da + jnp.dot(G[1].reshape(512, 1280), high, preferred_element_type=jnp.float32)
        DA[:, :, :n * HS] = da.astype(jnp.bfloat16).reshape(16, 32, n * HS)

    def backward(u, n):
        for h in range(n):
            lanes = columns(u + h, 1)
            for b in range(2):
                q = block_of(QKV.at[0], b, lanes)
                kk = block_of(QKV.at[1], b, lanes)
                v = block_of(QKV.at[2], b, lanes)
                d_att = block_of(DA, b, pl.ds(h * HS, HS))
                p = PR[2 * h + b]
                dp_ = lax.dot_general(d_att, v, (((1,), (1,)), ((), ())), preferred_element_type=jnp.float32)
                inner = jnp.sum(p * dp_, axis=-1, keepdims=True)
                ds = (p * (dp_ - inner)).astype(jnp.bfloat16)
                over_rows = (((0,), (0,)), ((), ()))
                dq = jnp.dot(ds, kk, preferred_element_type=jnp.float32) * (HS ** -0.5)
                dk = lax.dot_general(ds, q, over_rows, preferred_element_type=jnp.float32) * (HS ** -0.5)
                dv = lax.dot_general(p.astype(jnp.bfloat16), d_att, over_rows, preferred_element_type=jnp.float32)
                for dst, r in ((dq_out, dq), (dk_out, dk), (dv_out, dv)):
                    dst[0, :, pl.ds(16 * b, 16), lanes] = r.astype(jnp.bfloat16).reshape(16, 16, HS)

    def one(k, _):
        @pl.when(k >= 2)
        def _():
            head_rows(k - 2)

        drain(QKV.at[:, pl.ds(0, 14), :, columns(k, 1)], q_recv.at[k])

        @pl.when(k == heads - 1)
        def _():
            scatter_z(ASEND.at[0], ARECV.at[0], ar_send.at[0], ar_recv.at[0])

        @pl.when(k + AHEAD < heads)
        def _():
            send_group(k + AHEAD, k + AHEAD, 1)

        forward(k, 1)
        sum_cores(k, k, 1)
        to_xy(k, k, 1)

        @pl.when(k == heads - 1)
        def _():
            scatter_z(ASEND.at[1], ARECV.at[1], ar_send.at[1], ar_recv.at[1])

        @pl.when(k == 0)
        def _():
            drain(W.at[:, 1 - c], wf_recv)

        d_attended(k, 1)
        backward(k, 1)
        return 0

    lax.fori_loop(0, heads, one, 0)
    head_tiles(heads - 2, 0)

    def gather_rows(i):
        gather_z(ASEND.at[i], ARECV.at[i], AALL.at[i], ar_recv.at[i], ag_send.at[i], ag_recv.at[i])

    gather_rows(0)
    head_tiles(heads - 1, 1)
    scatter_z(BSEND, BRECV, br_send, br_recv)
    gather_rows(1)
    gather_z(BSEND, BRECV, BALL, br_recv, bg_send, bg_recv)
    for i in range(2):
        drain(AALL.at[i, pl.ds(0, 7)], ag_recv.at[i])
        for u in range(4):
            rows = AALL[i, 2 * u:2 * u + 2].astype(jnp.float32).reshape(160, HS)
            GW[:, (4 * i + u) * HS:(4 * i + u + 1) * HS] = rows * grad_scale
    drain(BALL.at[pl.ds(0, 7)], bg_recv)
    for h in range(2):
        for t in range(10):
            at = 10 * h + t
            lanes = pl.ds((8 + h) * HS, HS)
            GW[16 * t:16 * t + 16, lanes] = BALL[at // OWNED, at % OWNED].astype(jnp.float32) * grad_scale

    drain(G.at[m, pl.ds(0, 14)], g_send)
    drain(G.at[m], gy_send)
    drain(weight, wh_send)
    drain(W.at[pl.ds(0, 6), c], w_send)
    drain(W.at[:, c], wf_send)

    def settle(g, _):
        u, n = g, 1
        drain(QKV.at[:, pl.ds(0, 14), :, columns(u, n)], q_send.at[g])
        drain(CSEND.at[pl.ds(u, n)], c_send.at[g])
        drain(XSEND.at[pl.ds(u, n), pl.ds(0, 7)], x_send.at[g])
        return 0

    lax.fori_loop(0, heads, settle, 0)
    for i in range(2):
        drain(ARECV.at[i, pl.ds(0, 7)], ar_send.at[i])
        drain(ARECV.at[i, pl.ds(0, 7)], ag_send.at[i])
    drain(BRECV.at[pl.ds(0, 7)], br_send)
    drain(BRECV.at[pl.ds(0, 7)], bg_send)


def hand_on(*refs):
    sems = refs[8]
    copies = [
        pltpu.make_async_copy(s.at[0, pl.ds(8 * i, 8)], d.at[0, pl.ds(8 * i, 8)], sems.at[a, i])
        for a, (s, d) in enumerate(zip(refs[:3], refs[4:7]))
        for i in range(2)
    ]
    copies.append(pltpu.make_async_copy(refs[3], refs[7], sems.at[3, 0]))
    for copy in copies:
        copy.start()
    for copy in copies:
        copy.wait()


def on_device(query_heads, key_heads, value_heads, grad_out, out_weight):
    heads = query_heads.shape[3] // HS
    groups = heads
    bf, f32 = jnp.bfloat16, jnp.float32
    dma, vmem = pltpu.SemaphoreType.DMA, pltpu.VMEM
    anywhere = pl.BlockSpec(memory_space=pltpu.HBM)
    part = jax.ShapeDtypeStruct((1, 16, 32, 1280), bf)
    results = pl.pallas_call(
        functools.partial(kernel, heads, float(16 * 16 * 256) ** -0.5),
        out_shape=(part, part, part, jax.ShapeDtypeStruct((160, 1280), f32)),
        in_specs=[anywhere] * 5,
        out_specs=(pl.BlockSpec(memory_space=pltpu.VMEM),) * 4,
        scratch_shapes=[
            vmem((2, 16, 32, 1280), bf),
            vmem((2560, 512), bf),
            vmem((8, 2, 160, 1280), bf),
            vmem((3, 16, 32, 1280), bf),
            vmem((16, 32, HS), bf),
            vmem((16, 32, HS), bf),
            vmem((2, 256, 256), f32),
            vmem((256, 256), f32),
            vmem((heads, 8, 160, HS), bf),
            vmem((heads, 8, 160, HS), bf),
            vmem((1, 8, 160, HS), f32),
            vmem((heads, 8, 160, HS), bf),
            vmem((heads, 8, 160, HS), bf),
            vmem((2, 8, 80, HS), bf),
            vmem((2, 8, 80, HS), bf),
            vmem((2, 8, 80, HS), bf),
            vmem((8, OWNED, 16, HS), bf),
            vmem((8, OWNED, 16, HS), bf),
            vmem((8, OWNED, 16, HS), bf),
            dma, dma((7,)), dma, dma, dma, dma, dma, dma, dma, dma, dma((groups,)), dma((groups,)),
            dma, dma, dma, dma((groups,)), dma((groups,)), dma((groups,)), dma((groups,)),
            dma((2,)), dma((2,)), dma((2,)), dma((2,)), dma, dma, dma, dma,
        ],
        compiler_params=pltpu.CompilerParams(
            collective_id=0, has_side_effects=True, vmem_limit_bytes=49 * 2**20
        ),
    )(query_heads, key_heads, value_heads, grad_out, out_weight)
    return pl.pallas_call(
        hand_on,
        out_shape=(part, part, part, jax.ShapeDtypeStruct((160, 1280), f32)),
        in_specs=[pl.BlockSpec(memory_space=pl.ANY)] * 4,
        out_specs=(anywhere,) * 4,
        scratch_shapes=[dma((4, 2))],
        compiler_params=pltpu.CompilerParams(vmem_limit_bytes=2**20),
    )(*results)


def solution(mesh):
    placed = (
        P("dp", "tm", None, "mp"),
        P("dp", "tm", None, "mp"),
        P("dp", "tm", None, "mp"),
        P("dp", "tm", None, "mp"),
        P("dp", "mp"),
    )
    return jax.shard_map(
        on_device,
        mesh=mesh,
        in_specs=placed,
        out_specs=(
            P("dp", None, "tm", "mp"),
            P("dp", None, "tm", "mp"),
            P("dp", None, "tm", "mp"),
            P("dp", "mp"),
        ),
        check_vma=False,
    )
```
